128 devices in a mesh: shard: 16 (over z, y_hi, core), replica: 8 (over x, y_lo).
Axes of the slice: x: 4, y: 4 (y_hi: 2, y_lo: 2; y = y_hi * 2 + y_lo), z: 4, core: 2. Of those that a mesh axis runs over, the one named last changes fastest.
Arguments:
- tokens: bfloat16 [4096, 3072], P('replica'), may hold values from -6 to 6
- target: bfloat16 [4096, 3072], P('replica'), may hold values from -6 to 6
- w_in: bfloat16 [3072, 12288], P('replica', 'shard'), may hold values from -0.109375 to 0.109375
- probe_in: bfloat16 [3072, 12288], P('replica', 'shard'), may hold values from -1.5 to 1.5
- w_out: bfloat16 [3072, 12288], P('replica', 'shard'), may hold values from -0.0546875 to 0.0546875
- probe_out: bfloat16 [3072, 12288], P('replica', 'shard'), may hold values from -6 to 6
Outputs:
- grad_in: float32 [3072, 12288], P('replica', 'shard')
- hess_in: float32 [3072, 12288], P('replica', 'shard')
- grad_out: float32 [3072, 12288], P('replica', 'shard')
- hess_out: float32 [3072, 12288], P('replica', 'shard')
The draws below stay inside these ranges and needn't reach their ends.
All inputs are finite; a program needn't handle non-finite values.
Results may differ from the reference program's by a relative error of at most 0.025.
Values may be sent and summed in bfloat16 or wider, within the bound.
A program may use at most 192 MiB of HBM per device.

```python
import jax
import jax.numpy as jnp
from jax import lax

D = 3072
HID = 12288
TOK_REP = 512
TOKENS = 4096
N_REPLICA = 8


def strengthened(array, stream_key, source, target, parts, factor):
    def block_of(dim):
        return (jnp.arange(array.shape[dim]) // (array.shape[dim] // parts)).reshape((-1,) + (1,) * (array.ndim - 1 - dim))

    near = jax.random.permutation(stream_key, parts)[block_of(target)]
    second = (block_of(target) + parts // 2) % parts
    return jnp.where((block_of(source) == near) | (block_of(source) == second), factor * array, array)


def steps_of(key, extent, cuts, smallest, largest):
    def one(dim, shards_of):
        draws = jax.random.uniform(jax.random.fold_in(jax.random.fold_in(key, 6), dim), (shards_of,), jnp.float32, smallest / len(cuts), largest / len(cuts))
        return jnp.repeat(jnp.exp(draws), extent[dim] // shards_of).reshape((-1,) + (1,) * (len(extent) - dim - 1))

    loudness = one(*cuts[0])
    for cut in cuts[1:]:
        loudness = loudness * one(*cut)
    return loudness


def noise(own_key, dims, deviation, most, cuts=(), kind=jnp.bfloat16):
    loudness = steps_of(own_key, dims, cuts, -0.22, 0.18) if cuts else 1.0
    drawn = jax.random.normal(own_key, dims, jnp.float32) * deviation * loudness
    return jnp.minimum(jnp.maximum(drawn, -most), most).astype(kind)


def heavy_noise(stream_key, extent, spread, reach, cuts, heavy, dtype=jnp.bfloat16):
    array = spread * jax.random.normal(stream_key, extent, jnp.float32)
    if cuts:
        array = array * steps_of(stream_key, extent, cuts, -0.22, 0.18)
    return jnp.clip(strengthened(array, jax.random.fold_in(stream_key, 3), *heavy), -reach, reach).astype(dtype)


def setup_inputs(seed: int = 0) -> dict:
    seeds = jax.random.split(jax.random.key(seed), 7)
    return {
        "tokens": heavy_noise(seeds[0], (TOKENS, D), 1.0, 6.0, ((0, 8),), (0, 1, 8, 2.0)),
        "target": heavy_noise(seeds[1], (TOKENS, D), 1.0, 6.0, ((0, 8),), (0, 1, 8, 2.0)),
        "w_in": noise(seeds[2], (D, HID), D ** -0.5, 0.109375, ((0, 8), (1, 16))),
        "probe_in": noise(seeds[3], (D, HID), 0.25, 1.5, ((0, 8), (1, 16))),
        "w_out": noise(seeds[4], (D, HID), HID ** -0.5, 0.0546875, ((0, 8), (1, 16))),
        "probe_out": noise(seeds[5], (D, HID), 1.0, 6.0, ((0, 8), (1, 16))),
    }


def dot_f32(left, right):
    return jnp.dot(left, right, preferred_element_type=jnp.float32)


def reference(tokens, target, w_in, probe_in, w_out, probe_out):
    loss_scale = float(TOKENS) ** -0.5
    hidden_pre = dot_f32(tokens, w_in)
    pre_dot = dot_f32(tokens, probe_in)
    normal_cdf = 0.5 * (1.0 + jax.scipy.special.erf(hidden_pre * 0.7071067811865476))
    density = jnp.exp(-0.5 * hidden_pre * hidden_pre) * 0.3989422804014327
    first_deriv = normal_cdf + hidden_pre * density
    curve_term = density * (2.0 - hidden_pre * hidden_pre)
    activation = (hidden_pre * normal_cdf).astype(jnp.bfloat16)
    act_dot = (first_deriv * pre_dot).astype(jnp.bfloat16)
    output = dot_f32(activation, w_out.T)
    out_dot = dot_f32(act_dot, w_out.T) + dot_f32(activation, probe_out.T)
    error_term = (loss_scale * (output - target.astype(jnp.float32))).astype(jnp.bfloat16)
    error_dot = (loss_scale * out_dot).astype(jnp.bfloat16)
    back_grad = dot_f32(error_term, w_out)
    back_dot = dot_f32(error_dot, w_out) + dot_f32(error_term, probe_out)
    pre_grad = (back_grad * first_deriv).astype(jnp.bfloat16)
    pre_grad_dot = (back_dot * first_deriv + back_grad * curve_term * pre_dot).astype(jnp.bfloat16)

    def block_sums(carry, block):
        tok_blk, act_blk, actdot_blk, err_blk, errdot_blk, pg_blk, pgd_blk = block
        terms = (dot_f32(tok_blk.T, pg_blk), dot_f32(tok_blk.T, pgd_blk), dot_f32(err_blk.T, act_blk),
                 dot_f32(errdot_blk.T, act_blk) + dot_f32(err_blk.T, actdot_blk))
        rounded = tuple(term.astype(jnp.bfloat16) for term in terms)
        rounded = lax.optimization_barrier(rounded)
        return tuple(total + part.astype(jnp.float32) for total, part in zip(carry, rounded)), None

    arrays = (tokens, activation, act_dot, error_term, error_dot, pre_grad, pre_grad_dot)
    blocks = tuple(item.reshape(N_REPLICA, TOK_REP, item.shape[1]) for item in arrays)
    initial = tuple(jnp.zeros((D, HID), jnp.float32) for index_a in range(4))
    sums, unused = lax.scan(block_sums, initial, blocks)
    grad_in, hv_in, grad_out, hv_out = sums
    hess_in = loss_scale * probe_in.astype(jnp.float32) * hv_in
    hess_out = loss_scale * probe_out.astype(jnp.float32) * hv_out
    return grad_in, hess_in, grad_out, hess_out
```

```python
import functools

import jax
import jax.numpy as jnp
from jax import lax
from jax.experimental import pallas as pl
from jax.experimental.pallas import tpu as pltpu
from jax.sharding import PartitionSpec as P

MESH = pl.DeviceIdType.MESH
BF, F32 = jnp.bfloat16, jnp.float32
N_SEM = 160


def dot_nn(a, b):
    return jnp.dot(a, b, preferred_element_type=F32)


def dot_nt(a, b):
    return lax.dot_general(a, b, (((1,), (1,)), ((), ())), preferred_element_type=F32)


def dot_tn(a, b):
    return lax.dot_general(a, b, (((0,), (0,)), ((), ())), preferred_element_type=F32)


def block_kernel(
    scale, tok, tgt, w_in, p_in, w_out, p_out, out,
    Tk, Wi, Wo, acc, ad, fg, snd, sm, fr, fv, s2, sr, sv, err, xr, xv, ys, stage, tg, lsem, ssem, rsem,
):
    R = w_in.shape[0]
    H = w_in.shape[1] // 2
    T = tok.shape[0]
    K = 2 * R
    C = 2 * H

    shard, rep = lax.axis_index("shard"), lax.axis_index("replica")
    z, yh, c = shard // 4, (shard // 2) % 2, shard % 2
    x, l = rep // 2, rep % 2
    y = yh * 2 + l
    d = 1 - c

    def dev(x_, y_, z_, c_):
        x_, y_, z_ = x_ % 4, y_ % 4, z_ % 4
        return {"shard": z_ * 4 + (y_ // 2) * 2 + c_, "replica": x_ * 2 + y_ % 2}

    xp, xm = dev(x + 1, y, z, c), dev(x + 3, y, z, c)
    yp, ym = dev(x, y + 1, z, c), dev(x, y + 3, z, c)
    zp, zm = dev(x, y, z + 1, c), dev(x, y, z + 3, c)
    core = dev(x, y, z, d)
    mate = dev(x, yh * 2 + 1 - l, z, c)
    fp, fm = dev(x, y + c, z + d, c), dev(x, y + 3 * c, z + 3 * d, c)
    sp, sn = dev(x, y + d, z + c, c), dev(x, y + 3 * d, z + 3 * c, c)
    f, s = d * z + c * y, d * y + c * z

    barrier = pltpu.get_barrier_semaphore()
    for n in (xp, xm, yp, ym, zp, zm, core):
        pl.semaphore_signal(barrier, inc=1, device_id=n, device_id_type=MESH)
    pl.semaphore_wait(barrier, 7)

    ids = {}

    def copy(name, src, dst, to):
        n = ids.setdefault(name, len(ids))
        assert n < N_SEM
        cp = pltpu.make_async_remote_copy(
            src_ref=src, dst_ref=dst, send_sem=ssem.at[n], recv_sem=rsem.at[n], device_id=to, device_id_type=MESH
        )
        cp.start()
        return cp

    pending = []

    def send(name, src, dst, to):
        cp = copy(name, src, dst, to)
        pending.append(cp)
        return cp

    def al(v, m):
        return pl.multiple_of(v, m)

    def rows(i, n):
        return pl.ds(al(i * n, n), n)

    A, B = pl.ds(0, H), pl.ds(H, H)
    L, M = pl.ds(0, K), pl.ds(K, K)
    own, oth = rows(x * 2 + l, R), rows(x * 2 + 1 - l, R)

    def wrow(kx, lo):
        return rows((kx % 4) * 2 + lo, R)

    mine, theirs = rows(l, H), rows(1 - l, H)
    loc = []

    def local(src, dst):
        cp = pltpu.make_async_copy(src, dst, lsem.at[len(loc)])
        cp.start()
        loc.append(cp)
        return cp

    wi_loc = [local(w_in.at[:, mine], Wi.at[own, A]), local(p_in.at[:, mine], Wi.at[own, B])]
    yin = [send("yi0", w_in.at[:, theirs], Wi.at[own, A], mate), send("yi1", p_in.at[:, theirs], Wi.at[own, B], mate)]
    Q = T // 4
    tk = []
    for j, to in ((0, yp), (1, ym)):
        r = rows(2 * j + c, Q)
        tk.append(send("tk%d" % j, tok.at[r], Tk.at[pl.ds(al(l * T + (2 * j + c) * Q, Q), Q)], to))
    wo_loc = [local(w_out.at[:, mine], Wo.at[own, A]), local(p_out.at[:, mine], Wo.at[own, B])]
    tk_loc = local(tok, Tk.at[rows(l, T)])
    G = T // 16
    tg_loc = local(tgt.at[pl.ds(al(f * 4 * G + s * G, G), G)], tg.at[0])
    ym_ = yh * 2 + 1 - l
    f_, s_ = d * z + c * ym_, d * ym_ + c * z
    tgx = send("tg", tgt.at[pl.ds(al(f_ * 4 * G + s_ * G, G), G)], tg.at[1], mate)

    def ring1(tag, W, rws):
        return [send(tag + "p", W.at[rws], W.at[rws], xp), send(tag + "m", W.at[rws], W.at[rws], xm)]

    def ring2(tag, W, lo):
        a, b = wrow(x + 3, lo), wrow(x + 1, lo)
        return [send(tag + "p", W.at[a, A], W.at[a, A], xp), send(tag + "m", W.at[b, B], W.at[b, B], xm)]

    def got(cps):
        for cp in cps:
            cp.wait_recv()

    for cp in wi_loc:
        cp.wait()
    i1o = ring1("i1o", Wi, own)
    got(yin)
    i1t = ring1("i1t", Wi, oth)
    yout = [send("yo0", w_out.at[:, theirs], Wo.at[own, A], mate), send("yo1", p_out.at[:, theirs], Wo.at[own, B], mate)]
    got(i1o)
    i2o = ring2("i2o", Wi, l)
    got(tk)
    tc = []
    for j in (0, 1):
        r = pl.ds(al((1 - l) * T + (2 * j + c) * Q, Q), Q)
        tc.append(send("tc%d" % j, Tk.at[r], Tk.at[r], core))
    got(i1t)
    i2t = ring2("i2t", Wi, 1 - l)
    for cp in wo_loc:
        cp.wait()
    o1o = ring1("o1o", Wo, own)
    got(tc)
    tk_loc.wait()

    def pre_tile(r, kx):
        col = rows(kx % 4, K)
        return dot_nn(Tk[r, col], Wi[col, :])

    def pre_chunk(kx, first):
        @pl.loop(0, 4)
        def _(i):
            r = rows(i, 256)
            v = pre_tile(r, kx)
            acc[r, :] = v if first else acc[r, :] + v

    pre_chunk(x, True)
    got(yout)
    o1t = ring1("o1t", Wo, oth)
    pre_chunk(x + 1, False)
    pre_chunk(x + 3, False)
    got(i2o)
    got(i2t)

    @pl.loop(0, 8)
    def _(i):
        r = rows(i, 128)
        v = acc[r, :] + pre_tile(r, x + 2)
        h, pd = v[:, :H], v[:, H:]
        cdf = 0.5 * (1.0 + lax.erf(h * 0.7071067811865476))
        den = jnp.exp(-0.5 * h * h) * 0.3989422804014327
        fd = cdf + h * den
        ad[r, A] = (fd * pd).astype(BF)
        ad[r, B] = (h * cdf).astype(BF)
        fg[r, A] = fd
        fg[r, B] = den * (2.0 - h * h) * pd

    chunk = [x, x + 1, x + 3, x + 2]
    st = [dict() for _ in range(4)]

    def out_tile(i, r):
        w = rows(chunk[i] % 4, K)
        o = dot_nt(ad[r, B], Wo[w, A])
        t = dot_nt(ad[r, :], Wo[w, :])
        return o, t

    def sA(i):
        slot = i % 2
        if i >= 2:
            st[i - 2]["core"].wait_send()

        @pl.loop(0, T // 256)
        def _(j):
            o, t = out_tile(i, pl.ds(al(d * T + j * 256, 256), 256))
            snd[slot, rows(j, 256), L] = o.astype(BF)
            snd[slot, rows(j, 256), M] = t.astype(BF)

        st[i]["core"] = copy("ca%d" % i, snd.at[slot], sm.at[i], core)

    def sB(i):
        st[i]["core"].wait_recv()

        @pl.loop(0, T // 256)
        def _(j):
            o, t = out_tile(i, pl.ds(al(c * T + j * 256, 256), 256))
            r = rows(j, 256)
            sm[i, r, L] = (o + sm[i, r, L].astype(F32)).astype(BF)
            sm[i, r, M] = (t + sm[i, r, M].astype(F32)).astype(BF)

        r = rows((f + 2) % 4, 4 * G)
        st[i]["f1"] = [
            copy("fp%d" % i, sm.at[i, r, L], fr.at[i, 0], fp),
            copy("fm%d" % i, sm.at[i, r, M], fr.at[i, 1], fm),
        ]

    def add_to(buf, i, r, col, other):
        buf[i, r, col] = (buf[i, r, col].astype(F32) + other.astype(F32)).astype(BF)

    def sC(i):
        got(st[i]["f1"])
        rp, rm = rows((f + 1) % 4, 4 * G), rows((f + 3) % 4, 4 * G)
        add_to(sm, i, rp, L, fr[i, 0])
        add_to(sm, i, rm, M, fr[i, 1])
        st[i]["f2"] = [
            copy("gp%d" % i, sm.at[i, rp], fv.at[i, 0], fp),
            copy("gm%d" % i, sm.at[i, rm], fv.at[i, 1], fm),
        ]

    def sD(i):
        got(st[i]["f2"])
        r = rows(f, 4 * G)
        s2[i] = (sm[i, r, :].astype(F32) + fv[i, 0].astype(F32) + fv[i, 1].astype(F32)).astype(BF)
        r = rows((s + 2) % 4, G)
        st[i]["s1"] = [
            copy("sp%d" % i, s2.at[i, r, L], sr.at[i, 0], sp),
            copy("sn%d" % i, s2.at[i, r, M], sr.at[i, 1], sn),
        ]

    def sE(i):
        got(st[i]["s1"])
        rp, rm = rows((s + 1) % 4, G), rows((s + 3) % 4, G)
        add_to(s2, i, rp, L, sr[i, 0])
        add_to(s2, i, rm, M, sr[i, 1])
        st[i]["s2"] = [
            copy("tp%d" % i, s2.at[i, rp], sv.at[i, 0], sp),
            copy("tn%d" % i, s2.at[i, rm], sv.at[i, 1], sn),
        ]

    def erow(f_, s_):
        return pl.ds(al(c * T + f_ * (4 * G) + s_ * G, G), G)

    def frow(f_):
        return pl.ds(al(c * T + f_ * (4 * G), 4 * G), 4 * G)

    def sF(i):
        got(st[i]["s2"])
        v = s2[i, rows(s, G), :].astype(F32) + sv[i, 0].astype(F32) + sv[i, 1].astype(F32)
        e = erow(f, s)
        which = (l + c) % 2
        target = tg[which, :, rows(chunk[i] % 4, K)].astype(F32)
        err[i, e, L] = (scale * (v[:, :K] - target)).astype(BF)
        err[i, e, M] = (scale * v[:, K:]).astype(BF)
        st[i]["a1"] = [
            copy("up%d" % i, err.at[i, e], err.at[i, e], sp),
            copy("un%d" % i, err.at[i, e], err.at[i, e], sn),
        ]

    def sG(i):
        got(st[i]["a1"])
        a, b = erow(f, (s + 3) % 4), erow(f, (s + 1) % 4)
        st[i]["a2"] = [
            copy("vp%d" % i, err.at[i, a, L], err.at[i, a, L], sp),
            copy("vn%d" % i, err.at[i, b, M], err.at[i, b, M], sn),
        ]

    def sH(i):
        got(st[i]["a2"])
        e = frow(f)
        st[i]["b1"] = [
            copy("wp%d" % i, err.at[i, e], err.at[i, e], fp),
            copy("wm%d" % i, err.at[i, e], err.at[i, e], fm),
        ]

    def sI(i):
        got(st[i]["b1"])
        a, b = frow((f + 3) % 4), frow((f + 1) % 4)
        st[i]["b2"] = [
            copy("qp%d" % i, err.at[i, a, L], err.at[i, a, L], fp),
            copy("qm%d" % i, err.at[i, b, M], err.at[i, b, M], fm),
        ]

    def sJ(i):
        got(st[i]["b2"])
        e = rows(c, T)
        st[i]["c2"] = copy("cb%d" % i, err.at[i, e], err.at[i, e], core)

    lo_of = [1 - l, l]
    xs = {}

    def blk(q, i, h):
        lo = lo_of[h]
        if q == 0:
            return lambda col: sm.at[i, pl.ds(0, R), pl.ds(al(lo * C + col * H, H), H)]
        r = wrow(chunk[i], lo)
        return lambda col: Wi.at[r, pl.ds(col * H, H)]

    def x_far(q, h):
        b = blk(q, 3, h)
        xs[q, h, "r"] = [
            send("xr%d%dp" % (q, h), b(1), xr.at[q, h, 0], xp),
            send("xr%d%dm" % (q, h), b(0), xr.at[q, h, 1], xm),
        ]

    def x_near(q, h):
        xs[q, h, "n"] = [
            send("xn%d%dp" % (q, h), blk(q, 1, h)(0), xv.at[q, h, 0, :, A], xp),
            send("xn%d%dm" % (q, h), blk(q, 2, h)(1), xv.at[q, h, 1, :, B], xm),
        ]

    def x_relay(q, h):
        got(xs[q, h, "r"])
        pair = ((blk(q, 1, h)(1), 0), (blk(q, 2, h)(0), 1))

        @pl.loop(0, R // 128)
        def _(j):
            r = rows(j, 128)
            for ref, n in pair:
                ref[r, :] = (ref[r, :].astype(F32) + xr[q, h, n, r, :].astype(F32)).astype(BF)

        xs[q, h, "v"] = [
            send("xv%d%dp" % (q, h), pair[0][0], xv.at[q, h, 0, :, B], xp),
            send("xv%d%dm" % (q, h), pair[1][0], xv.at[q, h, 1, :, A], xm),
        ]

    def x_final(q, h):
        got(xs[q, h, "n"])
        got(xs[q, h, "v"])
        b = blk(q, 0, h)
        base = 2 * (1 - q)

        @pl.loop(0, R // 128)
        def _(j):
            r = rows(j, 128)
            for col, o in ((0, base + 1), (1, base)):
                cc = pl.ds(col * H, H)
                v = b(col)[r, :].astype(F32) + xv[q, h, 0, r, cc].astype(F32) + xv[q, h, 1, r, cc].astype(F32)
                if h == 0:
                    ys[q, r, cc] = v.astype(BF)
                else:
                    stage[o, r, mine] = v.astype(BF)

        if h == 0:
            xs[q, "y"] = [
                send("y%dh" % q, ys.at[q, :, A], stage.at[base + 1, :, mine], mate),
                send("y%dg" % q, ys.at[q, :, B], stage.at[base, :, mine], mate),
            ]

    def sK(i, first):
        st[i]["c2"].wait_recv()
        for name in ("f1", "f2"):
            for cp in st[i][name]:
                cp.wait_send()
        for h in (0, 1):
            lo = lo_of[h]

            @pl.loop(0, R // 128)
            def _(j):
                fc = al(lo * R + j * 128, 128)
                e = err[i, :, pl.ds(fc, 128)]
                ed = err[i, :, pl.ds(al(K + fc, 128), 128)]
                g = dot_tn(e, ad[...])
                hv = g[:, :H] + dot_tn(ed, ad[:, B])
                r = rows(j, 128)
                sm[i, r, pl.ds(al(lo * C, H), H)] = hv.astype(BF)
                sm[i, r, pl.ds(al(lo * C + H, H), H)] = g[:, H:].astype(BF)

            if i == 3:
                x_far(0, h)
        if i == 2:
            x_near(0, 0)
            x_near(0, 1)
        w = rows(chunk[i] % 4, K)

        @pl.loop(0, 4)
        def _(j):
            r = rows(j, 256)
            v = dot_nn(err[i, r, L], Wo[w, :])
            t = dot_nn(err[i, r, M], Wo[w, A])
            if first:
                acc[r, A] = v[:, :H]
                acc[r, B] = v[:, H:] + t
            else:
                acc[r, A] = acc[r, A] + v[:, :H]
                acc[r, B] = acc[r, B] + v[:, H:] + t

    o2 = {}

    def xo2(which):
        if which == 0:
            got(o1o)
            o2[0] = ring2("o2o", Wo, l)
        else:
            got(o1t)
            o2[1] = ring2("o2t", Wo, 1 - l)

    sA(0); sB(0); xo2(0); sC(0); sD(0); xo2(1)
    sA(1); sA(2); sE(0); sB(1); sB(2)
    tg_loc.wait()
    tgx.wait_recv()
    sF(0); sC(1); sC(2); sG(0); sD(1); sD(2); sH(0)
    got(o2[0]); got(o2[1])
    sA(3); sE(1); sE(2); sI(0); sB(3); sF(1); sF(2); sJ(0); sC(3); sG(1); sG(2); sD(3); sH(1); sH(2)
    sK(0, True); sE(3); sI(1); sI(2); sF(3); sJ(1); sJ(2); sG(3); sK(1, False); sH(3); sK(2, False); sI(3); sJ(3); sK(3, False)

    x_relay(0, 0)

    @pl.loop(0, 8)
    def _(j):
        r = rows(j, 128)
        bg, bd = acc[r, A], acc[r, B]
        fd = fg[r, A]
        ad[r, A] = (bd * fd + bg * fg[r, B]).astype(BF)
        ad[r, B] = (bg * fd).astype(BF)

    def part_in(i, h):
        lo = lo_of[h]

        @pl.loop(0, R // 128)
        def _(j):
            fc = al((chunk[i] % 4) * K + lo * R + j * 128, 128)
            v = dot_tn(Tk[:, pl.ds(fc, 128)], ad[...])
            Wi[pl.ds(fc, 128), :] = v.astype(BF)

    for cp in i1o + i1t + i2o + i2t:
        cp.wait_send()
    pending[:] = [cp for cp in pending if not any(cp is o for o in i1o + i1t + i2o + i2t)]
    part_in(3, 0)
    x_relay(0, 1)
    x_far(1, 0)
    part_in(1, 0)
    part_in(2, 0)
    x_near(1, 0)
    x_final(0, 0)
    part_in(0, 0)
    part_in(3, 1)
    x_far(1, 1)
    x_relay(1, 0)
    part_in(1, 1)
    part_in(2, 1)
    x_near(1, 1)
    part_in(0, 1)
    x_final(0, 1)
    x_relay(1, 1)
    x_final(1, 0)
    got(xs[0, "y"])
    o_out = local(stage.at[pl.ds(2, 2)], out.at[pl.ds(2, 2)])
    x_final(1, 1)
    got(xs[1, "y"])
    o_in = local(stage.at[pl.ds(0, 2)], out.at[pl.ds(0, 2)])
    for cp in pending:
        cp.wait_send()
    for i in range(4):
        for name in ("s1", "s2", "a1", "a2", "b1", "b2"):
            for cp in st[i][name]:
                cp.wait_send()
        st[i]["c2"].wait_send()
        if i >= 2:
            st[i]["core"].wait_send()
    o_out.wait()
    o_in.wait()


def on_device(tokens, target, w_in, probe_in, w_out, probe_out):
    R, hid = w_in.shape
    T, D = tokens.shape
    groups = lax.axis_size("replica")
    H, K, C = hid // 2, 2 * R, hid
    scale = float(T * groups) ** (-0.5)
    V = pltpu.VMEM
    scratch = [
        V((2 * T, D), BF),
        V((D, C), BF),
        V((D, C), BF),
        V((2 * T, C), F32),
        V((2 * T, C), BF),
        V((2 * T, C), F32),
        V((2, T, 2 * K), BF),
        V((4, T, 2 * K), BF),
        V((4, 2, T // 4, K), BF),
        V((4, 2, T // 4, 2 * K), BF),
        V((4, T // 4, 2 * K), BF),
        V((4, 2, T // 16, K), BF),
        V((4, 2, T // 16, 2 * K), BF),
        V((4, 2 * T, 2 * K), BF),
        V((2, 2, 2, R, H), BF),
        V((2, 2, 2, R, C), BF),
        V((2, R, C), BF),
        V((4, R, C), BF),
        V((2, T // 16, D), BF),
        pltpu.SemaphoreType.DMA((8,)),
        pltpu.SemaphoreType.DMA((N_SEM,)),
        pltpu.SemaphoreType.DMA((N_SEM,)),
    ]
    res = pl.pallas_call(
        functools.partial(block_kernel, scale),
        out_shape=jax.ShapeDtypeStruct((4, R, hid), BF),
        in_specs=[pl.BlockSpec(memory_space=pl.ANY)] * 6,
        out_specs=pl.BlockSpec(memory_space=pl.ANY),
        scratch_shapes=scratch,
        compiler_params=pltpu.CompilerParams(collective_id=0, has_side_effects=True, vmem_limit_bytes=64 * 2**20),
        cost_estimate=pl.CostEstimate(flops=26 * T * D * hid, bytes_accessed=40 * 2**20, transcendentals=4 * T * H),
        name="sophia_block",
    )(tokens, target, w_in, probe_in, w_out, probe_out)
    res = res.astype(F32)
    grad_in, hv_in, grad_out, hv_out = res[0], res[1], res[2], res[3]
    hess_in = scale * probe_in.astype(F32) * hv_in
    hess_out = scale * probe_out.astype(F32) * hv_out
    return grad_in, hess_in, grad_out, hess_out


def solution(mesh):
    wide = P("replica", "shard")
    return jax.shard_map(
        on_device,
        mesh=mesh,
        in_specs=(P("replica", None), P("replica", None), wide, wide, wide, wide),
        out_specs=(wide, wide, wide, wide),
        check_vma=False,
    )
```

```python
import functools

import jax
import jax.numpy as jnp
from jax import lax
from jax.experimental import pallas as pl
from jax.experimental.pallas import tpu as pltpu
from jax.sharding import PartitionSpec as P

MESH = pl.DeviceIdType.MESH
BF, F32 = jnp.bfloat16, jnp.float32
N_SEM = 240
SLOTS = 3
ORDER = (
    "A0", "A1", "A2", "Y3", "X4", "B0", "X5", "B1", "M0", "B2", "C0", "A3", "C1", "C2",
    "B3", "D0", "Y4", "D1", "D2", "C3", "E0", "E1", "E2", "Y5", "M1", "M2", "D3", "X6",
    "X7", "F0", "F1", "F2", "E3", "G0", "G1", "M3", "M4", "H0", "G2", "A4", "F3", "H1",
    "B4", "Y6", "I0", "H2", "G3", "I1", "C4", "J0", "A5", "I2", "H3", "Y7", "A6", "P0",
    "J1", "Q0", "D4", "B5", "J2", "B6", "I3", "E4", "A7", "P1", "C5", "P2", "C6", "B7",
    "F4", "J3", "Q2", "Q1", "D5", "P3", "D6", "Q3", "G4", "E5", "C7", "W0", "N1", "E6",
    "N6", "H4", "F5", "N2", "N4", "R0", "D7", "N3", "F6", "N0", "N7", "R1", "I4", "G5",
    "E7", "N5", "G6", "R4", "J4", "H5", "F7", "H6", "P4", "I5", "G7", "Q4", "T0", "I6",
    "J5", "H7", "R5", "J6", "P5", "I7", "Q5", "P6", "J7", "Q6", "T4", "T1", "P7", "T5",
    "Q7", "W1", "N12", "N14", "N15", "N11", "N9", "N13", "N8", "N10", "R2", "R3", "R6", "R7",
    "T2", "T3", "T6", "T7",
)
FIRST = {next(int(t[1:]) for t in ORDER if t[0] == "Q" and (int(t[1:]) >= 4) == a) for a in (False, True)}


class Copy:
    def __init__(self, cp):
        self.cp, self.sent, self.landed = cp, False, False
        cp.start()

    def wait_send(self):
        if not self.sent:
            self.cp.wait_send()
        self.sent = True

    def wait_recv(self):
        if not self.landed:
            self.cp.wait_recv()
        self.landed = True


def dot_nn(a, b):
    return jnp.dot(a, b, preferred_element_type=F32)


def dot_nt(a, b):
    return lax.dot_general(a, b, (((1,), (1,)), ((), ())), preferred_element_type=F32)


def dot_tn(a, b):
    return lax.dot_general(a, b, (((0,), (0,)), ((), ())), preferred_element_type=F32)


def block_kernel(
    scale, tok, tgt, w_in, p_in, w_out, p_out, out0, out1, out2, out3,
    Tk, Wi, Wo, acc, ad, fg, pg, snd, sm, fr, fv, s2, sr, sv, err, xr, xv, ys, stage, tg, lsem, ssem, rsem,
):
    R = w_in.shape[0]
    H = w_in.shape[1] // 2
    T = tok.shape[0]
    K = 2 * R
    C = 2 * H

    shard, rep = lax.axis_index("shard"), lax.axis_index("replica")
    z, yh, c = shard // 4, (shard // 2) % 2, shard % 2
    x, l = rep // 2, rep % 2
    y = yh * 2 + l
    d = 1 - c

    def dev(x_, y_, z_, c_):
        x_, y_, z_ = x_ % 4, y_ % 4, z_ % 4
        return {"shard": z_ * 4 + (y_ // 2) * 2 + c_, "replica": x_ * 2 + y_ % 2}

    xp, xm = dev(x + 1, y, z, c), dev(x + 3, y, z, c)
    yp, ym = dev(x, y + 1, z, c), dev(x, y + 3, z, c)
    zp, zm = dev(x, y, z + 1, c), dev(x, y, z + 3, c)
    core = dev(x, y, z, d)
    mate = dev(x, yh * 2 + 1 - l, z, c)
    fp, fm = dev(x, y + c, z + d, c), dev(x, y + 3 * c, z + 3 * d, c)
    sp, sn = dev(x, y + d, z + c, c), dev(x, y + 3 * d, z + 3 * c, c)
    f, s = d * z + c * y, d * y + c * z

    barrier = pltpu.get_barrier_semaphore()
    for n in (xp, xm, yp, ym, zp, zm, core):
        pl.semaphore_signal(barrier, inc=1, device_id=n, device_id_type=MESH)
    pl.semaphore_wait(barrier, 7)

    ids = {}

    started = []

    def send(name, src, dst, to):
        n = ids.setdefault(name, len(ids))
        assert n < N_SEM
        cp = Copy(pltpu.make_async_remote_copy(
            src_ref=src, dst_ref=dst, send_sem=ssem.at[n], recv_sem=rsem.at[n], device_id=to, device_id_type=MESH
        ))
        started.append(cp)
        return cp

    def al(v, m):
        return pl.multiple_of(v, m)

    def rows(i, n):
        return pl.ds(al(i * n, n), n)

    A, B = pl.ds(0, H), pl.ds(H, H)
    L, M = pl.ds(0, R), pl.ds(R, R)
    own, oth = rows(x * 2 + l, R), rows(x * 2 + 1 - l, R)

    mine, theirs = rows(l, H), rows(1 - l, H)
    loc = []

    def local(src, dst):
        cp = pltpu.make_async_copy(src, dst, lsem.at[len(loc)])
        cp.start()
        loc.append(cp)
        return cp

    def got(cps):
        for cp in cps:
            cp.wait_recv()

    arrays = ((w_in, Wi, A), (w_out, Wo, A), (p_in, Wi, B), (p_out, Wo, B))
    yx = {}

    def swap(n):
        src, W, col = arrays[n]
        yx[n] = send("yx%d" % n, src.at[:, theirs], W.at[own, col], mate)

    wl = [local(src.at[:, mine], W.at[own, col]) for src, W, col in arrays]
    swap(0)
    far = dev(x, y + 3 + 2 * l, z, c)
    Q = T // 32
    parts = ((0, 5 * Q, mate), (10 * Q, 11 * Q, far))
    tk = []
    for j, (at, n, to) in enumerate(parts):
        r = pl.ds(al(at + c * n, Q), n)
        tk.append(send("tk%d" % j, tok.at[r], Tk.at[pl.ds(al(l * T + at + c * n, Q), n)], to))
    tk_loc = local(tok, Tk.at[rows(l, T)])
    swap(1)
    G = T // 16
    tg_loc = local(tgt.at[pl.ds(al(f * 4 * G + s * G, G), G)], tg.at[0])
    ym_ = yh * 2 + 1 - l
    f_, s_ = d * z + c * ym_, d * ym_ + c * z
    tgx = send("tg", tgt.at[pl.ds(al(f_ * 4 * G + s_ * G, G), G)], tg.at[1], mate)

    top, bot = pl.ds(0, R // 2), pl.ds(R // 2, R // 2)
    r1, r2 = {}, {}

    def half_rows(kx, lo, k):
        return pl.ds(al((kx % 4) * K + lo * R + k * (R // 2), R // 2), R // 2)

    def ring1(n, h):
        _, W, col = arrays[n]
        if h:
            got([yx[n]])
        else:
            wl[n].wait()
        b = W.at[oth if h else own, col]
        r1[n, h] = [send("r1%d%dp" % (n, h), b, b, xp), send("r1%d%dm" % (n, h), b, b, xm)]

    def ring2(n, h):
        _, W, col = arrays[n]
        got(r1[n, h])
        lo = 1 - l if h else l
        a, b = W.at[half_rows(x + 3, lo, 1), col], W.at[half_rows(x + 1, lo, 0), col]
        r2[n, h] = [send("r2%d%dp" % (n, h), a, a, xp), send("r2%d%dm" % (n, h), b, b, xm)]

    def pre_rows(half, kx, col, first):
        r, w = rows(half, T), rows(kx % 4, K)
        v = dot_nn(Tk[r, w], Wi[w, col])
        acc[r, col] = v if first else acc[r, col] + v

    def activate(half):
        @pl.loop(0, T // 128)
        def _(i):
            r = pl.ds(al(half * T + i * 128, 128), 128)
            h = acc[r, A]
            cdf = 0.5 * (1.0 + lax.erf(h * 0.7071067811865476))
            den = jnp.exp(-0.5 * h * h) * 0.3989422804014327
            ad[r, B] = (h * cdf).astype(BF)
            fg[r, A] = cdf + h * den
            fg[r, B] = den * (2.0 - h * h)

    chunk = [x, x + 1, x + 3, x + 2]
    ring1(0, 0)
    ring1(0, 1)
    ring2(0, 0)
    ring2(0, 1)
    ring1(1, 0)
    tk_loc.wait()
    for i in range(3):
        pre_rows(l, chunk[i], A, i == 0)
    got(r2[0, 0])
    got(r2[0, 1])
    pre_rows(l, chunk[3], A, False)
    got(tk)
    tc = []
    for j, (at, n, _) in enumerate(parts):
        r = pl.ds(al((1 - l) * T + at + c * n, Q), n)
        tc.append(send("tc%d" % j, Tk.at[r], Tk.at[r], core))
    swap(2)
    swap(3)
    activate(l)
    ring1(1, 1)
    ring2(1, 0)
    got(tc)
    for i in range(4):
        pre_rows(1 - l, chunk[i], A, i == 0)
    activate(1 - l)

    def tangent(i):
        if i in (1, 2):
            got(r1[2, 0])
            got(r1[2, 1])
        if i == 3:
            got(r2[2, 0])
            got(r2[2, 1])
        if i < 4:
            for half in (0, 1):
                pre_rows(half, chunk[i], B, i == 0)
            return

        @pl.loop(0, 2 * T // 128)
        def _(i):
            r = rows(i, 128)
            pd = acc[r, B]
            ad[r, A] = (fg[r, A] * pd).astype(BF)
            fg[r, B] = fg[r, B] * pd

    st = [dict() for _ in range(8)]

    def wrows(u):
        return rows(chunk[u % 4] % 4, K)

    def out_half(u, half):
        r, w = rows(half, T), wrows(u)
        if u < 4:
            return dot_nt(ad[r, B], Wo[w, A])
        return dot_nt(ad[r, :], Wo[w, :])

    def sA(u):
        n = 1 if u < 4 else 3
        if u % 4 in (1, 2):
            got(r1[n, 0])
            got(r1[n, 1])
        if u % 4 == 3:
            got(r2[n, 0])
            got(r2[n, 1])
        if u >= SLOTS:
            st[u - SLOTS]["core"].wait_send()
        snd[u % SLOTS] = out_half(u, d).astype(BF)
        st[u]["core"] = send("ca%d" % u, snd.at[u % SLOTS], sm.at[u], core)

    def sB(u):
        o = out_half(u, c)
        st[u]["core"].wait_recv()
        sm[u] = (o + sm[u].astype(F32)).astype(BF)
        r = rows((f + 2) % 4, 4 * G)
        st[u]["f1"] = [
            send("fp%d" % u, sm.at[u, r, L], fr.at[u, 0], fp),
            send("fm%d" % u, sm.at[u, r, M], fr.at[u, 1], fm),
        ]

    def add_to(buf, i, r, col, other):
        buf[i, r, col] = (buf[i, r, col].astype(F32) + other.astype(F32)).astype(BF)

    def sC(i):
        got(st[i]["f1"])
        rp, rm = rows((f + 1) % 4, 4 * G), rows((f + 3) % 4, 4 * G)
        add_to(sm, i, rp, L, fr[i, 0])
        add_to(sm, i, rm, M, fr[i, 1])
        st[i]["f2"] = [
            send("gp%d" % i, sm.at[i, rp], fv.at[i, 0], fp),
            send("gm%d" % i, sm.at[i, rm], fv.at[i, 1], fm),
        ]

    def sD(i):
        got(st[i]["f2"])
        r = rows(f, 4 * G)
        s2[i] = (sm[i, r, :].astype(F32) + fv[i, 0].astype(F32) + fv[i, 1].astype(F32)).astype(BF)
        r = rows((s + 2) % 4, G)
        st[i]["s1"] = [
            send("sp%d" % i, s2.at[i, r, L], sr.at[i, 0], sp),
            send("sn%d" % i, s2.at[i, r, M], sr.at[i, 1], sn),
        ]

    def sE(i):
        got(st[i]["s1"])
        rp, rm = rows((s + 1) % 4, G), rows((s + 3) % 4, G)
        add_to(s2, i, rp, L, sr[i, 0])
        add_to(s2, i, rm, M, sr[i, 1])
        st[i]["s2"] = [
            send("tp%d" % i, s2.at[i, rp], sv.at[i, 0], sp),
            send("tn%d" % i, s2.at[i, rm], sv.at[i, 1], sn),
        ]

    def erow(f_, s_):
        return pl.ds(al(c * T + f_ * (4 * G) + s_ * G, G), G)

    def frow(f_):
        return pl.ds(al(c * T + f_ * (4 * G), 4 * G), 4 * G)

    def sF(i):
        got(st[i]["s2"])
        v = s2[i, rows(s, G), :].astype(F32) + sv[i, 0].astype(F32) + sv[i, 1].astype(F32)
        e = erow(f, s)
        if i < 4:
            v = v - tg[(l + c) % 2, :, wrows(i)].astype(F32)
        err[i, e, :] = (scale * v).astype(BF)
        st[i]["a1"] = [
            send("up%d" % i, err.at[i, e], err.at[i, e], sp),
            send("un%d" % i, err.at[i, e], err.at[i, e], sn),
        ]

    def sG(i):
        got(st[i]["a1"])
        a, b = erow(f, (s + 3) % 4), erow(f, (s + 1) % 4)
        st[i]["a2"] = [
            send("vp%d" % i, err.at[i, a, L], err.at[i, a, L], sp),
            send("vn%d" % i, err.at[i, b, M], err.at[i, b, M], sn),
        ]

    def sH(i):
        got(st[i]["a2"])
        e = frow(f)
        st[i]["b1"] = [
            send("wp%d" % i, err.at[i, e], err.at[i, e], fp),
            send("wm%d" % i, err.at[i, e], err.at[i, e], fm),
        ]

    def sI(i):
        got(st[i]["b1"])
        a, b = frow((f + 3) % 4), frow((f + 1) % 4)
        st[i]["b2"] = [
            send("qp%d" % i, err.at[i, a, L], err.at[i, a, L], fp),
            send("qm%d" % i, err.at[i, b, M], err.at[i, b, M], fm),
        ]

    def sJ(i):
        got(st[i]["b2"])
        e = rows(c, T)
        st[i]["c2"] = send("cb%d" % i, err.at[i, e], err.at[i, e], core)

    lo_of = (1 - l, l)
    xs = {}

    def blk(q, a, i, h, part=None):
        lo = lo_of[h]
        k, n = {None: (0, R), 0: (0, R // 2), 1: (R // 2, R // 2)}[part]
        if q == 0:
            return sm.at[4 * a + i, pl.ds(k, n), pl.ds(al(lo * H, H), H)]
        return Wi.at[pl.ds(al((chunk[i] % 4) * K + lo * R + k, n), n), pl.ds(a * H, H)]

    def unit(q, a, h):
        return q * 4 + a * 2 + h

    def x_out(q, a, i, h):
        n = unit(q, a, h)
        if i == 3:
            xs[n, "r"] = [
                send("xr%dp" % n, blk(q, a, 3, h, 1), xr.at[n, 0], xp),
                send("xr%dm" % n, blk(q, a, 3, h, 0), xr.at[n, 1], xm),
            ]
        elif i == 1:
            xs[n, "np"] = send("xn%dp" % n, blk(q, a, 1, h, 0), xv.at[n, 0, top], xp)
        elif i == 2:
            xs[n, "nm"] = send("xn%dm" % n, blk(q, a, 2, h, 1), xv.at[n, 1, bot], xm)

    def x_relay(n):
        q, a, h = n // 4, (n // 2) % 2, n % 2
        got(xs[n, "r"])
        up, down = blk(q, a, 1, h, 1), blk(q, a, 2, h, 0)
        up[...] = (up[...].astype(F32) + xr[n, 0].astype(F32)).astype(BF)
        down[...] = (down[...].astype(F32) + xr[n, 1].astype(F32)).astype(BF)
        xs[n, "v"] = [send("xv%dp" % n, up, xv.at[n, 0, bot], xp), send("xv%dm" % n, down, xv.at[n, 1, top], xm)]

    def x_final(n):
        q, a, h = n // 4, (n // 2) % 2, n % 2
        got([xs[n, "np"], xs[n, "nm"]] + xs[n, "v"])
        v = (blk(q, a, 0, h)[...].astype(F32) + xv[n, 0].astype(F32) + xv[n, 1].astype(F32)).astype(BF)
        o = 2 * (1 - q) + a
        if h:
            stage[o, :, mine] = v
        else:
            ys[o] = v
            xs[o, "y"] = send("y%d" % o, ys.at[o], stage.at[o, :, mine], mate)

    def sP(u):
        st[u]["c2"].wait_recv()
        for name in ("f1", "f2"):
            for cp in st[u][name]:
                cp.wait_send()
        for h in (0, 1):
            cols = rows(lo_of[h], H)
            g = dot_tn(err[u, :, cols], ad[:, B])
            if u >= 4:
                g = g + dot_tn(err[u - 4, :, cols], ad[:, A])
            sm[u, pl.ds(0, R), cols] = g.astype(BF)
            x_out(0, u // 4, u % 4, h)

    def sQ(u):
        st[u]["c2"].wait_recv()
        w = wrows(u)

        @pl.loop(0, 2 * T // 512)
        def _(j):
            r = rows(j, 512)
            v = dot_nn(err[u, r, :], Wo[w, A])
            if u >= 4:
                v = v + dot_nn(err[u - 4, r, :], Wo[w, B])
            col = B if u >= 4 else A
            acc[r, col] = v if u in FIRST else acc[r, col] + v

    def pre_grad(a):
        @pl.loop(0, 2 * T // 128)
        def _(j):
            r = rows(j, 128)
            if a:
                ad[r, A] = (acc[r, B] * fg[r, A] + acc[r, A] * fg[r, B]).astype(BF)
            else:
                pg[r, :] = (acc[r, A] * fg[r, A]).astype(BF)

        for cp in r1[2 * a, 0] + r1[2 * a, 1] + r2[2 * a, 0] + r2[2 * a, 1]:
            cp.wait_send()

    def sN(n):
        a, i, h = n // 8, (n // 2) % 4, n % 2
        fc = pl.ds(al((chunk[i] % 4) * K + lo_of[h] * R, R), R)
        right = ad[:, A] if a else pg[...]
        Wi[fc, pl.ds(a * H, H)] = dot_tn(Tk[:, fc], right).astype(BF)
        x_out(1, a, i, h)

    def sF0(u):
        if u == 0:
            tg_loc.wait()
            tgx.wait_recv()
        sF(u)

    tasks = {
        "A": sA, "B": sB, "C": sC, "D": sD, "E": sE, "F": sF0, "G": sG, "H": sH, "I": sI, "J": sJ, "P": sP, "Q": sQ,
        "X": lambda n: ring1(n // 2, n % 2), "Y": lambda n: ring2(n // 2, n % 2), "M": tangent, "R": x_relay,
        "T": x_final, "W": pre_grad, "N": sN,
    }
    for step in ORDER:
        tasks[step[0]](int(step[1:]))
    got([xs[2, "y"], xs[3, "y"]])
    fin = [local(stage.at[2], out2), local(stage.at[3], out3)]
    got([xs[0, "y"], xs[1, "y"]])
    fin += [local(stage.at[0], out0), local(stage.at[1], out1)]
    for cp in started:
        cp.wait_send()
    for cp in fin:
        cp.wait()


def on_device(tokens, target, w_in, probe_in, w_out, probe_out):
    R, hid = w_in.shape
    T, D = tokens.shape
    groups = lax.axis_size("replica")
    H, K, C = hid // 2, 2 * R, hid
    scale = float(T * groups) ** (-0.5)
    V = pltpu.VMEM
    scratch = [
        V((2 * T, D), BF),
        V((D, C), BF),
        V((D, C), BF),
        V((2 * T, C), F32),
        V((2 * T, C), BF),
        V((2 * T, C), F32),
        V((2 * T, H), BF),
        V((SLOTS, T, K), BF),
        V((8, T, K), BF),
        V((8, 2, T // 4, R), BF),
        V((8, 2, T // 4, K), BF),
        V((8, T // 4, K), BF),
        V((8, 2, T // 16, R), BF),
        V((8, 2, T // 16, K), BF),
        V((8, 2 * T, K), BF),
        V((8, 2, R // 2, H), BF),
        V((8, 2, R, H), BF),
        V((4, R, H), BF),
        V((4, R, C), BF),
        V((2, T // 16, D), BF),
        pltpu.SemaphoreType.DMA((12,)),
        pltpu.SemaphoreType.DMA((N_SEM,)),
        pltpu.SemaphoreType.DMA((N_SEM,)),
    ]
    grad_in, hv_in, grad_out, hv_out = pl.pallas_call(
        functools.partial(block_kernel, scale),
        out_shape=(jax.ShapeDtypeStruct((R, hid), BF),) * 4,
        in_specs=[pl.BlockSpec(memory_space=pl.ANY)] * 6,
        out_specs=(pl.BlockSpec(memory_space=pl.ANY),) * 4,
        scratch_shapes=scratch,
        compiler_params=pltpu.CompilerParams(collective_id=0, has_side_effects=True, vmem_limit_bytes=64 * 2**20),
        cost_estimate=pl.CostEstimate(flops=26 * T * D * hid, bytes_accessed=40 * 2**20, transcendentals=4 * T * H),
        name="sophia_block",
    )(tokens, target, w_in, probe_in, w_out, probe_out)
    hess_in = scale * probe_in.astype(F32) * hv_in.astype(F32)
    hess_out = scale * probe_out.astype(F32) * hv_out.astype(F32)
    return grad_in.astype(F32), hess_in, grad_out.astype(F32), hess_out


def solution(mesh):
    wide = P("replica", "shard")
    return jax.shard_map(
        on_device,
        mesh=mesh,
        in_specs=(P("replica", None), P("replica", None), wide, wide, wide, wide),
        out_specs=(wide, wide, wide, wide),
        check_vma=False,
    )
```

```python
import functools

import jax
import jax.numpy as jnp
from jax import lax
from jax.experimental import pallas as pl
from jax.experimental.pallas import tpu as pltpu
from jax.sharding import PartitionSpec as P

MESH = pl.DeviceIdType.MESH
BF, F32 = jnp.bfloat16, jnp.float32
N_SEM = 240
SLOTS = 3
ORDER = (
    "A0", "A1", "Y3", "B0", "A2", "X4", "X5", "B1", "M0", "C0", "B2", "A3", "C1", "D0",
    "B3", "C2", "Y4", "D1", "E0", "C3", "D2", "E1", "F0", "Y5", "M1", "E2", "F1", "G0",
    "X6", "X7", "D3", "M2", "F2", "G1", "H0", "E3", "M3", "G2", "H1", "M4", "A4", "I0",
    "F3", "H2", "B4", "Y6", "J0", "I1", "G3", "I2", "P0", "Q0", "J1", "H3", "C4", "A5",
    "J2", "Y7", "A6", "P1", "Q1", "I3", "B5", "P2", "D4", "A7", "B6", "C5", "J3", "Q2",
    "E4", "B7", "C6", "P3", "Q3", "D5", "F4", "W0", "N1", "C7", "N0", "N6", "D6", "E5",
    "N4", "R0", "G4", "N5", "N3", "N7", "E6", "D7", "F5", "R1", "H4", "N2", "F6", "E7",
    "G5", "R4", "I4", "G6", "F7", "T0", "H5", "J4", "H6", "G7", "I5", "P4", "R5", "I6",
    "H7", "Q4", "J5", "T1", "J6", "P5", "I7", "P6", "Q6", "J7", "Q5", "T5", "T4", "P7",
    "Q7", "W1", "N14", "N10", "N12", "R2", "R3", "N8", "R6", "N15", "N11", "N13", "N9", "T2",
    "T3", "T6", "R7", "T7",
)
FIRST = {next(int(t[1:]) for t in ORDER if t[0] == "Q" and (int(t[1:]) >= 4) == a) for a in (False, True)}


class Copy:
    def __init__(self, cp):
        self.cp, self.sent, self.landed = cp, False, False
        cp.start()

    def wait_send(self):
        if not self.sent:
            self.cp.wait_send()
        self.sent = True

    def wait_recv(self):
        if not self.landed:
            self.cp.wait_recv()
        self.landed = True


def dot_nn(a, b):
    return jnp.dot(a, b, preferred_element_type=F32)


def dot_nt(a, b):
    return lax.dot_general(a, b, (((1,), (1,)), ((), ())), preferred_element_type=F32)


def dot_tn(a, b):
    return lax.dot_general(a, b, (((0,), (0,)), ((), ())), preferred_element_type=F32)


def block_kernel(
    scale, tok, tgt, w_in, p_in, w_out, p_out, out0, out1, out2, out3,
    Tk, Wi, Wo, acc, ad, fg, pg, snd, sm, fr, fv, s2, sr, sv, err, xr, xv, ys, stage, tg, lsem, ssem, rsem,
):
    R = w_in.shape[0]
    H = w_in.shape[1] // 2
    T = tok.shape[0]
    K = 2 * R
    C = 2 * H

    shard, rep = lax.axis_index("shard"), lax.axis_index("replica")
    z, yh, c = shard // 4, (shard // 2) % 2, shard % 2
    x, l = rep // 2, rep % 2
    y = yh * 2 + l
    d = 1 - c

    def dev(x_, y_, z_, c_):
        x_, y_, z_ = x_ % 4, y_ % 4, z_ % 4
        return {"shard": z_ * 4 + (y_ // 2) * 2 + c_, "replica": x_ * 2 + y_ % 2}

    xp, xm = dev(x + 1, y, z, c), dev(x + 3, y, z, c)
    yp, ym = dev(x, y + 1, z, c), dev(x, y + 3, z, c)
    zp, zm = dev(x, y, z + 1, c), dev(x, y, z + 3, c)
    core = dev(x, y, z, d)
    mate = dev(x, yh * 2 + 1 - l, z, c)
    fp, fm = dev(x, y + c, z + d, c), dev(x, y + 3 * c, z + 3 * d, c)
    sp, sn = dev(x, y + d, z + c, c), dev(x, y + 3 * d, z + 3 * c, c)
    f, s = d * z + c * y, d * y + c * z

    barrier = pltpu.get_barrier_semaphore()
    for n in (xp, xm, yp, ym, zp, zm, core):
        pl.semaphore_signal(barrier, inc=1, device_id=n, device_id_type=MESH)
    pl.semaphore_wait(barrier, 7)

    ids = {}

    started = []

    def send(name, src, dst, to):
        n = ids.setdefault(name, len(ids))
        assert n < N_SEM
        cp = Copy(pltpu.make_async_remote_copy(
            src_ref=src, dst_ref=dst, send_sem=ssem.at[n], recv_sem=rsem.at[n], device_id=to, device_id_type=MESH
        ))
        started.append(cp)
        return cp

    def al(v, m):
        return pl.multiple_of(v, m)

    def rows(i, n):
        return pl.ds(al(i * n, n), n)

    A, B = pl.ds(0, H), pl.ds(H, H)
    L, M = pl.ds(0, R), pl.ds(R, R)
    own, oth = rows(x * 2 + l, R), rows(x * 2 + 1 - l, R)

    mine, theirs = rows(l, H), rows(1 - l, H)
    loc = []

    def local(src, dst):
        cp = pltpu.make_async_copy(src, dst, lsem.at[len(loc)])
        cp.start()
        loc.append(cp)
        return cp

    def got(cps):
        for cp in cps:
            cp.wait_recv()

    arrays = ((w_in, Wi, A), (w_out, Wo, A), (p_in, Wi, B), (p_out, Wo, B))
    yx = {}

    def swap(n):
        src, W, col = arrays[n]
        yx[n] = send("yx%d" % n, src.at[:, theirs], W.at[own, col], mate)

    r1, r2 = {}, {}
    r1[0, 0] = [send("r100p", w_in.at[:, mine], Wi.at[own, A], xp), send("r100m", w_in.at[:, mine], Wi.at[own, A], xm)]
    swap(0)
    far = dev(x, y + 3 + 2 * l, z, c)
    Q = T // 32
    parts = ((10 * Q, 6 * Q, far), (0, 5 * Q, mate), (22 * Q, 5 * Q, far))
    tk = {}

    def send_tokens(j):
        at, n, to = parts[j]
        r = pl.ds(al(at + c * n, Q), n)
        tk[j] = send("tk%d" % j, tok.at[r], Tk.at[pl.ds(al(l * T + at + c * n, Q), n)], to)

    send_tokens(0)
    send_tokens(2)
    wl = [local(src.at[:, mine], W.at[own, col]) for src, W, col in arrays]
    tk_loc = local(tok, Tk.at[rows(l, T)])
    G = T // 16
    tg_loc = local(tgt.at[pl.ds(al(f * 4 * G + s * G, G), G)], tg.at[0])
    ym_ = yh * 2 + 1 - l
    f_, s_ = d * z + c * ym_, d * ym_ + c * z

    top, bot = pl.ds(0, R // 2), pl.ds(R // 2, R // 2)

    def half_rows(kx, lo, k):
        return pl.ds(al((kx % 4) * K + lo * R + k * (R // 2), R // 2), R // 2)

    def ring1(n, h):
        _, W, col = arrays[n]
        if h:
            got([yx[n]])
        else:
            wl[n].wait()
        if h and n == 2:
            swap(3)
        b = W.at[oth if h else own, col]
        r1[n, h] = [send("r1%d%dp" % (n, h), b, b, xp), send("r1%d%dm" % (n, h), b, b, xm)]

    def ring2(n, h):
        _, W, col = arrays[n]
        got(r1[n, h])
        lo = 1 - l if h else l
        a, b = W.at[half_rows(x + 3, lo, 1), col], W.at[half_rows(x + 1, lo, 0), col]
        r2[n, h] = [send("r2%d%dp" % (n, h), a, a, xp), send("r2%d%dm" % (n, h), b, b, xm)]

    def pre_rows(half, kx, col, first):
        r, w = rows(half, T), rows(kx % 4, K)
        v = dot_nn(Tk[r, w], Wi[w, col])
        acc[r, col] = v if first else acc[r, col] + v

    def activate(half):
        @pl.loop(0, T // 128)
        def _(i):
            r = pl.ds(al(half * T + i * 128, 128), 128)
            h = acc[r, A]
            cdf = 0.5 * (1.0 + lax.erf(h * 0.7071067811865476))
            den = jnp.exp(-0.5 * h * h) * 0.3989422804014327
            ad[r, B] = (h * cdf).astype(BF)
            fg[r, A] = cdf + h * den
            fg[r, B] = den * (2.0 - h * h)

    chunk = [x, x + 1, x + 3, x + 2]
    ring1(0, 1)
    send_tokens(1)
    swap(1)
    ring2(0, 0)
    ring2(0, 1)
    wl[0].wait()
    tk_loc.wait()
    for i in range(3):
        pre_rows(l, chunk[i], A, i == 0)
    got(r2[0, 0])
    ring1(1, 0)
    got(r2[0, 1])
    pre_rows(l, chunk[3], A, False)
    activate(l)
    tc = []
    for j, (at, n, _) in enumerate(parts):
        got([tk[j]])
        r = pl.ds(al((1 - l) * T + at + c * n, Q), n)
        tc.append(send("tc%d" % j, Tk.at[r], Tk.at[r], core))
        if j == 1:
            ring1(1, 1)
            ring2(1, 0)
    tgx = send("tg", tgt.at[pl.ds(al(f_ * 4 * G + s_ * G, G), G)], tg.at[1], mate)
    swap(2)
    got(tc)
    for i in range(4):
        pre_rows(1 - l, chunk[i], A, i == 0)
    activate(1 - l)

    def tangent(i):
        if i in (1, 2):
            got(r1[2, 0])
            got(r1[2, 1])
        if i == 3:
            got(r2[2, 0])
            got(r2[2, 1])
        if i < 4:
            for half in (0, 1):
                pre_rows(half, chunk[i], B, i == 0)
            return

        @pl.loop(0, 2 * T // 128)
        def _(i):
            r = rows(i, 128)
            pd = acc[r, B]
            ad[r, A] = (fg[r, A] * pd).astype(BF)
            fg[r, B] = fg[r, B] * pd

    st = [dict() for _ in range(8)]

    def wrows(u):
        return rows(chunk[u % 4] % 4, K)

    def out_half(u, half):
        r, w = rows(half, T), wrows(u)
        if u < 4:
            return dot_nt(ad[r, B], Wo[w, A])
        return dot_nt(ad[r, :], Wo[w, :])

    def sA(u):
        n = 1 if u < 4 else 3
        if u % 4 in (1, 2):
            got(r1[n, 0])
            got(r1[n, 1])
        if u % 4 == 3:
            got(r2[n, 0])
            got(r2[n, 1])
        if u >= SLOTS:
            st[u - SLOTS]["core"].wait_send()
        snd[u % SLOTS] = out_half(u, d).astype(BF)
        st[u]["core"] = send("ca%d" % u, snd.at[u % SLOTS], sm.at[u], core)

    def sB(u):
        o = out_half(u, c)
        st[u]["core"].wait_recv()
        sm[u] = (o + sm[u].astype(F32)).astype(BF)
        r = rows((f + 2) % 4, 4 * G)
        st[u]["f1"] = [
            send("fp%d" % u, sm.at[u, r, L], fr.at[u, 0], fp),
            send("fm%d" % u, sm.at[u, r, M], fr.at[u, 1], fm),
        ]

    def add_to(buf, i, r, col, other):
        buf[i, r, col] = (buf[i, r, col].astype(F32) + other.astype(F32)).astype(BF)

    def sC(i):
        got(st[i]["f1"])
        rp, rm = rows((f + 1) % 4, 4 * G), rows((f + 3) % 4, 4 * G)
        add_to(sm, i, rp, L, fr[i, 0])
        add_to(sm, i, rm, M, fr[i, 1])
        st[i]["f2"] = [
            send("gp%d" % i, sm.at[i, rp], fv.at[i, 0], fp),
            send("gm%d" % i, sm.at[i, rm], fv.at[i, 1], fm),
        ]

    def sD(i):
        got(st[i]["f2"])
        r = rows(f, 4 * G)
        s2[i] = (sm[i, r, :].astype(F32) + fv[i, 0].astype(F32) + fv[i, 1].astype(F32)).astype(BF)
        r = rows((s + 2) % 4, G)
        st[i]["s1"] = [
            send("sp%d" % i, s2.at[i, r, L], sr.at[i, 0], sp),
            send("sn%d" % i, s2.at[i, r, M], sr.at[i, 1], sn),
        ]

    def sE(i):
        got(st[i]["s1"])
        rp, rm = rows((s + 1) % 4, G), rows((s + 3) % 4, G)
        add_to(s2, i, rp, L, sr[i, 0])
        add_to(s2, i, rm, M, sr[i, 1])
        st[i]["s2"] = [
            send("tp%d" % i, s2.at[i, rp], sv.at[i, 0], sp),
            send("tn%d" % i, s2.at[i, rm], sv.at[i, 1], sn),
        ]

    def erow(f_, s_):
        return pl.ds(al(c * T + f_ * (4 * G) + s_ * G, G), G)

    def frow(f_):
        return pl.ds(al(c * T + f_ * (4 * G), 4 * G), 4 * G)

    def sF(i):
        got(st[i]["s2"])
        v = s2[i, rows(s, G), :].astype(F32) + sv[i, 0].astype(F32) + sv[i, 1].astype(F32)
        e = erow(f, s)
        if i < 4:
            v = v - tg[(l + c) % 2, :, wrows(i)].astype(F32)
        err[i, e, :] = (scale * v).astype(BF)
        st[i]["a1"] = [
            send("up%d" % i, err.at[i, e], err.at[i, e], sp),
            send("un%d" % i, err.at[i, e], err.at[i, e], sn),
        ]

    def sG(i):
        got(st[i]["a1"])
        a, b = erow(f, (s + 3) % 4), erow(f, (s + 1) % 4)
        st[i]["a2"] = [
            send("vp%d" % i, err.at[i, a, L], err.at[i, a, L], sp),
            send("vn%d" % i, err.at[i, b, M], err.at[i, b, M], sn),
        ]

    def sH(i):
        got(st[i]["a2"])
        e = frow(f)
        st[i]["b1"] = [
            send("wp%d" % i, err.at[i, e], err.at[i, e], fp),
            send("wm%d" % i, err.at[i, e], err.at[i, e], fm),
        ]

    def sI(i):
        got(st[i]["b1"])
        a, b = frow((f + 3) % 4), frow((f + 1) % 4)
        st[i]["b2"] = [
            send("qp%d" % i, err.at[i, a, L], err.at[i, a, L], fp),
            send("qm%d" % i, err.at[i, b, M], err.at[i, b, M], fm),
        ]

    def sJ(i):
        got(st[i]["b2"])
        e = rows(c, T)
        st[i]["c2"] = send("cb%d" % i, err.at[i, e], err.at[i, e], core)

    lo_of = (1 - l, l)
    xs = {}

    def blk(q, a, i, h, part=None):
        lo = lo_of[h]
        k, n = {None: (0, R), 0: (0, R // 2), 1: (R // 2, R // 2)}[part]
        if q == 0:
            return sm.at[4 * a + i, pl.ds(k, n), pl.ds(al(lo * H, H), H)]
        if a and i == 0:
            return pg.at[pl.ds(h * R + k, n)]
        return Wi.at[pl.ds(al((chunk[i] % 4) * K + lo * R + k, n), n), pl.ds(a * H, H)]

    def unit(q, a, h):
        return q * 4 + a * 2 + h

    def x_out(q, a, i, h):
        n = unit(q, a, h)
        if i == 3:
            xs[n, "r"] = [
                send("xr%dp" % n, blk(q, a, 3, h, 1), xr.at[n, 0], xp),
                send("xr%dm" % n, blk(q, a, 3, h, 0), xr.at[n, 1], xm),
            ]
        elif i == 1:
            xs[n, "np"] = send("xn%dp" % n, blk(q, a, 1, h, 0), xv.at[n, 0, top], xp)
        elif i == 2:
            xs[n, "nm"] = send("xn%dm" % n, blk(q, a, 2, h, 1), xv.at[n, 1, bot], xm)

    def x_relay(n):
        q, a, h = n // 4, (n // 2) % 2, n % 2
        got(xs[n, "r"])
        up, down = blk(q, a, 1, h, 1), blk(q, a, 2, h, 0)
        up[...] = (up[...].astype(F32) + xr[n, 0].astype(F32)).astype(BF)
        down[...] = (down[...].astype(F32) + xr[n, 1].astype(F32)).astype(BF)
        xs[n, "v"] = [send("xv%dp" % n, up, xv.at[n, 0, bot], xp), send("xv%dm" % n, down, xv.at[n, 1, top], xm)]

    def x_final(n):
        q, a, h = n // 4, (n // 2) % 2, n % 2
        got([xs[n, "np"], xs[n, "nm"]] + xs[n, "v"])
        v = blk(q, a, 0, h)[...].astype(F32) + xv[n, 0].astype(F32) + xv[n, 1].astype(F32)
        if a:
            probe = (Wi if q else Wo)[rows(x * 2 + lo_of[h], R), B]
            v = scale * probe.astype(F32) * v
        v = v.astype(BF)
        o = 2 * (1 - q) + a
        if h:
            stage[o, :, mine] = v
        else:
            ys[o] = v
            xs[o, "y"] = send("y%d" % o, ys.at[o], stage.at[o, :, mine], mate)

    def sP(u):
        st[u]["c2"].wait_recv()
        for name in ("f1", "f2"):
            for cp in st[u][name]:
                cp.wait_send()
        for h in (0, 1):
            cols = rows(lo_of[h], H)
            g = dot_tn(err[u, :, cols], ad[:, B])
            if u >= 4:
                g = g + dot_tn(err[u - 4, :, cols], ad[:, A])
            sm[u, pl.ds(0, R), cols] = g.astype(BF)
            x_out(0, u // 4, u % 4, h)

    def sQ(u):
        st[u]["c2"].wait_recv()
        w = wrows(u)
        col = B if u >= 4 else A
        v = dot_nn(err[u], Wo[w, A])
        acc[:, col] = v if u in FIRST else acc[:, col] + v
        if u >= 4:
            acc[:, col] = acc[:, col] + dot_nn(err[u - 4], Wo[w, B])

    def pre_grad(a):
        @pl.loop(0, 2 * T // 128)
        def _(j):
            r = rows(j, 128)
            if a:
                ad[r, A] = (acc[r, B] * fg[r, A] + acc[r, A] * fg[r, B]).astype(BF)
            else:
                pg[r, :] = (acc[r, A] * fg[r, A]).astype(BF)

        for cp in r1[2 * a, 0] + r1[2 * a, 1] + r2[2 * a, 0] + r2[2 * a, 1]:
            cp.wait_send()

    def sN(n):
        a, i, h = n // 8, (n // 2) % 4, n % 2
        fc = pl.ds(al((chunk[i] % 4) * K + lo_of[h] * R, R), R)
        right = ad[:, A] if a else pg[...]
        blk(1, a, i, h)[...] = dot_tn(Tk[:, fc], right).astype(BF)
        x_out(1, a, i, h)

    def sF0(u):
        if u == 0:
            tg_loc.wait()
            tgx.wait_recv()
        sF(u)

    tasks = {
        "A": sA, "B": sB, "C": sC, "D": sD, "E": sE, "F": sF0, "G": sG, "H": sH, "I": sI, "J": sJ, "P": sP, "Q": sQ,
        "X": lambda n: ring1(n // 2, n % 2), "Y": lambda n: ring2(n // 2, n % 2), "M": tangent, "R": x_relay,
        "T": x_final, "W": pre_grad, "N": sN,
    }
    for step in ORDER:
        tasks[step[0]](int(step[1:]))
    got([xs[2, "y"], xs[3, "y"]])
    fin = [local(stage.at[2], out2), local(stage.at[3], out3)]
    got([xs[0, "y"], xs[1, "y"]])
    fin += [local(stage.at[0], out0), local(stage.at[1], out1)]
    for cp in started:
        cp.wait_send()
    for cp in fin:
        cp.wait()


def on_device(tokens, target, w_in, probe_in, w_out, probe_out):
    R, hid = w_in.shape
    T, D = tokens.shape
    groups = lax.axis_size("replica")
    H, K, C = hid // 2, 2 * R, hid
    scale = float(T * groups) ** (-0.5)
    V = pltpu.VMEM
    scratch = [
        V((2 * T, D), BF),
        V((D, C), BF),
        V((D, C), BF),
        V((2 * T, C), F32),
        V((2 * T, C), BF),
        V((2 * T, C), F32),
        V((2 * T, H), BF),
        V((SLOTS, T, K), BF),
        V((8, T, K), BF),
        V((8, 2, T // 4, R), BF),
        V((8, 2, T // 4, K), BF),
        V((8, T // 4, K), BF),
        V((8, 2, T // 16, R), BF),
        V((8, 2, T // 16, K), BF),
        V((8, 2 * T, K), BF),
        V((8, 2, R // 2, H), BF),
        V((8, 2, R, H), BF),
        V((4, R, H), BF),
        V((4, R, C), BF),
        V((2, T // 16, D), BF),
        pltpu.SemaphoreType.DMA((12,)),
        pltpu.SemaphoreType.DMA((N_SEM,)),
        pltpu.SemaphoreType.DMA((N_SEM,)),
    ]
    res = pl.pallas_call(
        functools.partial(block_kernel, scale),
        out_shape=(jax.ShapeDtypeStruct((R, hid), BF),) * 4,
        in_specs=[pl.BlockSpec(memory_space=pl.ANY)] * 6,
        out_specs=(pl.BlockSpec(memory_space=pl.ANY),) * 4,
        scratch_shapes=scratch,
        compiler_params=pltpu.CompilerParams(collective_id=0, has_side_effects=True, vmem_limit_bytes=64 * 2**20),
        cost_estimate=pl.CostEstimate(flops=26 * T * D * hid, bytes_accessed=40 * 2**20, transcendentals=4 * T * H),
        name="sophia_block",
    )(tokens, target, w_in, probe_in, w_out, probe_out)
    return tuple(v.astype(F32) for v in res)


def solution(mesh):
    wide = P("replica", "shard")
    return jax.shard_map(
        on_device,
        mesh=mesh,
        in_specs=(P("replica", None), P("replica", None), wide, wide, wide, wide),
        out_specs=(wide, wide, wide, wide),
        check_vma=False,
    )
```

```python
import functools

import jax
import jax.numpy as jnp
from jax import lax
from jax.experimental import pallas as pl
from jax.experimental.pallas import tpu as pltpu
from jax.sharding import PartitionSpec as P

MESH = pl.DeviceIdType.MESH
BF, F32 = jnp.bfloat16, jnp.float32
N_SEM = 240
SLOTS = 3
ORDER = (
    "A0", "A1", "Y3", "B0", "A2", "X4", "X5", "B1", "M0", "C0", "B2", "A3", "C1", "D0",
    "B3", "C2", "Y4", "D1", "E0", "C3", "D2", "E1", "F0", "Y5", "M1", "E2", "F1", "G0",
    "X6", "X7", "D3", "M2", "F2", "G1", "H0", "E3", "M3", "G2", "H1", "M4", "A4", "I0",
    "F3", "H2", "B4", "Y6", "J0", "I1", "G3", "I2", "P0", "Q0", "J1", "H3", "C4", "A5",
    "J2", "Y7", "A6", "P1", "Q1", "I3", "B5", "P2", "D4", "A7", "B6", "C5", "J3", "Q2",
    "E4", "B7", "C6", "P3", "Q3", "D5", "F4", "W0", "N1", "C7", "N0", "N6", "D6", "E5",
    "N4", "R0", "G4", "N5", "N3", "N7", "E6", "D7", "F5", "R1", "H4", "N2", "F6", "E7",
    "G5", "R4", "I4", "G6", "F7", "T0", "H5", "J4", "H6", "G7", "I5", "P4", "R5", "I6",
    "H7", "Q4", "J5", "T1", "J6", "P5", "I7", "P6", "Q6", "J7", "Q5", "T5", "T4", "P7",
    "Q7", "W1", "N14", "N10", "N12", "R2", "R3", "N8", "R6", "N15", "N11", "N13", "N9", "T2",
    "T3", "T6", "R7", "T7",
)
FIRST = {next(int(t[1:]) for t in ORDER if t[0] == "Q" and (int(t[1:]) >= 4) == a) for a in (False, True)}


class Copy:
    def __init__(self, cp):
        self.cp, self.sent, self.landed = cp, False, False
        cp.start()

    def wait_send(self):
        if not self.sent:
            self.cp.wait_send()
        self.sent = True

    def wait_recv(self):
        if not self.landed:
            self.cp.wait_recv()
        self.landed = True


def dot_nn(a, b):
    return jnp.dot(a, b, preferred_element_type=F32)


def dot_nt(a, b):
    return lax.dot_general(a, b, (((1,), (1,)), ((), ())), preferred_element_type=F32)


def dot_tn(a, b):
    return lax.dot_general(a, b, (((0,), (0,)), ((), ())), preferred_element_type=F32)


def block_kernel(
    scale, tok, tgt, w_in, p_in, w_out, p_out, out0, out1, out2, out3,
    Tk, Wi, Wo, acc, ad, fg, pg, snd, sm, fr, fv, s2, sr, sv, err, xr, xv, ys, stage, tg, lsem, ssem, rsem,
):
    R = w_in.shape[0]
    H = w_in.shape[1] // 2
    T = tok.shape[0]
    K = 2 * R
    C = 2 * H

    shard, rep = lax.axis_index("shard"), lax.axis_index("replica")
    z, yh, c = shard // 4, (shard // 2) % 2, shard % 2
    x, l = rep // 2, rep % 2
    y = yh * 2 + l
    d = 1 - c

    def dev(x_, y_, z_, c_):
        x_, y_, z_ = x_ % 4, y_ % 4, z_ % 4
        return {"shard": z_ * 4 + (y_ // 2) * 2 + c_, "replica": x_ * 2 + y_ % 2}

    xp, xm = dev(x + 1, y, z, c), dev(x + 3, y, z, c)
    yp, ym = dev(x, y + 1, z, c), dev(x, y + 3, z, c)
    zp, zm = dev(x, y, z + 1, c), dev(x, y, z + 3, c)
    core = dev(x, y, z, d)
    mate = dev(x, yh * 2 + 1 - l, z, c)
    fp, fm = dev(x, y + c, z + d, c), dev(x, y + 3 * c, z + 3 * d, c)
    sp, sn = dev(x, y + d, z + c, c), dev(x, y + 3 * d, z + 3 * c, c)
    f, s = d * z + c * y, d * y + c * z

    barrier = pltpu.get_barrier_semaphore()
    for n in (xp, xm, yp, ym, zp, zm, core):
        pl.semaphore_signal(barrier, inc=1, device_id=n, device_id_type=MESH)
    pl.semaphore_wait(barrier, 7)

    ids = {}

    started = []

    def send(name, src, dst, to):
        n = ids.setdefault(name, len(ids))
        assert n < N_SEM
        cp = Copy(pltpu.make_async_remote_copy(
            src_ref=src, dst_ref=dst, send_sem=ssem.at[n], recv_sem=rsem.at[n], device_id=to, device_id_type=MESH
        ))
        started.append(cp)
        return cp

    def al(v, m):
        return pl.multiple_of(v, m)

    def rows(i, n):
        return pl.ds(al(i * n, n), n)

    A, B = pl.ds(0, H), pl.ds(H, H)
    L, M = pl.ds(0, R), pl.ds(R, R)
    own, oth = rows(x * 2 + l, R), rows(x * 2 + 1 - l, R)

    mine, theirs = rows(l, H), rows(1 - l, H)
    loc = []

    def local(src, dst):
        cp = pltpu.make_async_copy(src, dst, lsem.at[len(loc)])
        cp.start()
        loc.append(cp)
        return cp

    def got(cps):
        for cp in cps:
            cp.wait_recv()

    arrays = ((w_in, Wi, A), (w_out, Wo, A), (p_in, Wi, B), (p_out, Wo, B))
    yx = {}

    def swap(n):
        src, W, col = arrays[n]
        yx[n] = send("yx%d" % n, src.at[:, theirs], W.at[own, col], mate)

    r1, r2 = {}, {}
    r1[0, 0] = [send("r100p", w_in.at[:, mine], Wi.at[own, A], xp), send("r100m", w_in.at[:, mine], Wi.at[own, A], xm)]
    swap(0)
    far = dev(x, y + 3 + 2 * l, z, c)
    Q = T // 32
    parts = ((10 * Q, 6 * Q, far), (0, 5 * Q, mate), (22 * Q, 5 * Q, far))
    tk = {}

    def send_tokens(j):
        at, n, to = parts[j]
        r = pl.ds(al(at + c * n, Q), n)
        tk[j] = send("tk%d" % j, tok.at[r], Tk.at[pl.ds(al(l * T + at + c * n, Q), n)], to)

    send_tokens(0)
    send_tokens(2)
    wl = [local(src.at[:, mine], W.at[own, col]) for src, W, col in arrays]
    tk_loc = local(tok, Tk.at[rows(l, T)])
    G = T // 16
    tg_loc = local(tgt.at[pl.ds(al(f * 4 * G + s * G, G), G)], tg.at[0])
    ym_ = yh * 2 + 1 - l
    f_, s_ = d * z + c * ym_, d * ym_ + c * z

    top, bot = pl.ds(0, R // 2), pl.ds(R // 2, R // 2)

    def half_rows(kx, lo, k):
        return pl.ds(al((kx % 4) * K + lo * R + k * (R // 2), R // 2), R // 2)

    def ring1(n, h):
        _, W, col = arrays[n]
        if h:
            got([yx[n]])
        else:
            wl[n].wait()
        if h and n == 2:
            swap(3)
        b = W.at[oth if h else own, col]
        r1[n, h] = [send("r1%d%dp" % (n, h), b, b, xp), send("r1%d%dm" % (n, h), b, b, xm)]

    def ring2(n, h):
        _, W, col = arrays[n]
        got(r1[n, h])
        lo = 1 - l if h else l
        a, b = W.at[half_rows(x + 3, lo, 1), col], W.at[half_rows(x + 1, lo, 0), col]
        r2[n, h] = [send("r2%d%dp" % (n, h), a, a, xp), send("r2%d%dm" % (n, h), b, b, xm)]

    def pre_rows(half, kx, col, first):
        r, w = rows(half, T), rows(kx % 4, K)
        v = dot_nn(Tk[r, w], Wi[w, col])
        acc[r, col] = v if first else acc[r, col] + v

    def activate(half):
        @pl.loop(0, T // 128)
        def _(i):
            r = pl.ds(al(half * T + i * 128, 128), 128)
            h = acc[r, A]
            cdf = 0.5 * (1.0 + lax.erf(h * 0.7071067811865476))
            den = jnp.exp(-0.5 * h * h) * 0.3989422804014327
            ad[r, B] = (h * cdf).astype(BF)
            fg[r, A] = cdf + h * den
            fg[r, B] = den * (2.0 - h * h)

    chunk = [x, x + 1, x + 3, x + 2]
    ring1(0, 1)
    send_tokens(1)
    swap(1)
    ring2(0, 0)
    ring2(0, 1)
    wl[0].wait()
    tk_loc.wait()
    for i in range(3):
        pre_rows(l, chunk[i], A, i == 0)
    got(r2[0, 0])
    ring1(1, 0)
    got(r2[0, 1])
    pre_rows(l, chunk[3], A, False)
    activate(l)
    tc = []
    for j, (at, n, _) in enumerate(parts):
        got([tk[j]])
        r = pl.ds(al((1 - l) * T + at + c * n, Q), n)
        tc.append(send("tc%d" % j, Tk.at[r], Tk.at[r], core))
        if j == 1:
            ring1(1, 1)
            ring2(1, 0)
    tgx = send("tg", tgt.at[pl.ds(al(f_ * 4 * G + s_ * G, G), G)], tg.at[1], mate)
    swap(2)
    got(tc)
    for i in range(4):
        pre_rows(1 - l, chunk[i], A, i == 0)
    activate(1 - l)

    def tangent(i):
        if i in (1, 2):
            got(r1[2, 0])
            got(r1[2, 1])
        if i == 3:
            got(r2[2, 0])
            got(r2[2, 1])
        if i < 4:
            for half in (0, 1):
                pre_rows(half, chunk[i], B, i == 0)
            return

        @pl.loop(0, 2 * T // 128)
        def _(i):
            r = rows(i, 128)
            pd = acc[r, B]
            ad[r, A] = (fg[r, A] * pd).astype(BF)
            fg[r, B] = fg[r, B] * pd

    st = [dict() for _ in range(8)]

    def wrows(u):
        return rows(chunk[u % 4] % 4, K)

    def out_half(u, half):
        r, w = rows(half, T), wrows(u)
        if u < 4:
            return dot_nt(ad[r, B], Wo[w, A])
        return dot_nt(ad[r, :], Wo[w, :])

    def sA(u):
        n = 1 if u < 4 else 3
        if u % 4 in (1, 2):
            got(r1[n, 0])
            got(r1[n, 1])
        if u % 4 == 3:
            got(r2[n, 0])
            got(r2[n, 1])
        if u >= SLOTS:
            st[u - SLOTS]["core"].wait_send()
        snd[u % SLOTS] = out_half(u, d).astype(BF)
        st[u]["core"] = send("ca%d" % u, snd.at[u % SLOTS], sm.at[u], core)

    def sB(u):
        o = out_half(u, c)
        st[u]["core"].wait_recv()
        sm[u] = (o + sm[u].astype(F32)).astype(BF)
        r = rows((f + 2) % 4, 4 * G)
        st[u]["f1"] = [
            send("fp%d" % u, sm.at[u, r, L], fr.at[u, 0], fp),
            send("fm%d" % u, sm.at[u, r, M], fr.at[u, 1], fm),
        ]

    def add_to(buf, i, r, col, other):
        buf[i, r, col] = (buf[i, r, col].astype(F32) + other.astype(F32)).astype(BF)

    def sC(i):
        got(st[i]["f1"])
        rp, rm = rows((f + 1) % 4, 4 * G), rows((f + 3) % 4, 4 * G)
        add_to(sm, i, rp, L, fr[i, 0])
        add_to(sm, i, rm, M, fr[i, 1])
        st[i]["f2"] = [
            send("gp%d" % i, sm.at[i, rp], fv.at[i, 0], fp),
            send("gm%d" % i, sm.at[i, rm], fv.at[i, 1], fm),
        ]

    def sD(i):
        got(st[i]["f2"])
        r = rows(f, 4 * G)
        s2[i] = (sm[i, r, :].astype(F32) + fv[i, 0].astype(F32) + fv[i, 1].astype(F32)).astype(BF)
        r = rows((s + 2) % 4, G)
        st[i]["s1"] = [
            send("sp%d" % i, s2.at[i, r, L], sr.at[i, 0], sp),
            send("sn%d" % i, s2.at[i, r, M], sr.at[i, 1], sn),
        ]

    def sE(i):
        got(st[i]["s1"])
        rp, rm = rows((s + 1) % 4, G), rows((s + 3) % 4, G)
        add_to(s2, i, rp, L, sr[i, 0])
        add_to(s2, i, rm, M, sr[i, 1])
        st[i]["s2"] = [
            send("tp%d" % i, s2.at[i, rp], sv.at[i, 0], sp),
            send("tn%d" % i, s2.at[i, rm], sv.at[i, 1], sn),
        ]

    def erow(f_, s_):
        return pl.ds(al(c * T + f_ * (4 * G) + s_ * G, G), G)

    def frow(f_):
        return pl.ds(al(c * T + f_ * (4 * G), 4 * G), 4 * G)

    def sF(i):
        got(st[i]["s2"])
        v = s2[i, rows(s, G), :].astype(F32) + sv[i, 0].astype(F32) + sv[i, 1].astype(F32)
        e = erow(f, s)
        if i < 4:
            v = v - tg[(l + c) % 2, :, wrows(i)].astype(F32)
        err[i, e, :] = (scale * v).astype(BF)
        st[i]["a1"] = [
            send("up%d" % i, err.at[i, e], err.at[i, e], sp),
            send("un%d" % i, err.at[i, e], err.at[i, e], sn),
        ]

    def sG(i):
        got(st[i]["a1"])
        a, b = erow(f, (s + 3) % 4), erow(f, (s + 1) % 4)
        st[i]["a2"] = [
            send("vp%d" % i, err.at[i, a, L], err.at[i, a, L], sp),
            send("vn%d" % i, err.at[i, b, M], err.at[i, b, M], sn),
        ]

    def sH(i):
        got(st[i]["a2"])
        e = frow(f)
        st[i]["b1"] = [
            send("wp%d" % i, err.at[i, e], err.at[i, e], fp),
            send("wm%d" % i, err.at[i, e], err.at[i, e], fm),
        ]

    def sI(i):
        got(st[i]["b1"])
        a, b = frow((f + 3) % 4), frow((f + 1) % 4)
        st[i]["b2"] = [
            send("qp%d" % i, err.at[i, a, L], err.at[i, a, L], fp),
            send("qm%d" % i, err.at[i, b, M], err.at[i, b, M], fm),
        ]

    def sJ(i):
        got(st[i]["b2"])
        e = rows(c, T)
        st[i]["c2"] = send("cb%d" % i, err.at[i, e], err.at[i, e], core)

    lo_of = (1 - l, l)
    xs = {}

    def blk(q, a, i, h, part=None):
        lo = lo_of[h]
        k, n = {None: (0, R), 0: (0, R // 2), 1: (R // 2, R // 2)}[part]
        if q == 0:
            return sm.at[4 * a + i, pl.ds(k, n), pl.ds(al(lo * H, H), H)]
        if a and i == 0:
            return pg.at[pl.ds(h * R + k, n)]
        return Wi.at[pl.ds(al((chunk[i] % 4) * K + lo * R + k, n), n), pl.ds(a * H, H)]

    def unit(q, a, h):
        return q * 4 + a * 2 + h

    def x_out(q, a, i, h):
        n = unit(q, a, h)
        if i == 3:
            xs[n, "r"] = [
                send("xr%dp" % n, blk(q, a, 3, h, 1), xr.at[n, 0], xp),
                send("xr%dm" % n, blk(q, a, 3, h, 0), xr.at[n, 1], xm),
            ]
        elif i == 1:
            xs[n, "np"] = send("xn%dp" % n, blk(q, a, 1, h, 0), xv.at[n, 0, top], xp)
        elif i == 2:
            xs[n, "nm"] = send("xn%dm" % n, blk(q, a, 2, h, 1), xv.at[n, 1, bot], xm)

    def x_relay(n):
        q, a, h = n // 4, (n // 2) % 2, n % 2
        got(xs[n, "r"])
        up, down = blk(q, a, 1, h, 1), blk(q, a, 2, h, 0)
        up[...] = (up[...].astype(F32) + xr[n, 0].astype(F32)).astype(BF)
        down[...] = (down[...].astype(F32) + xr[n, 1].astype(F32)).astype(BF)
        xs[n, "v"] = [send("xv%dp" % n, up, xv.at[n, 0, bot], xp), send("xv%dm" % n, down, xv.at[n, 1, top], xm)]

    def x_final(n):
        q, a, h = n // 4, (n // 2) % 2, n % 2
        got([xs[n, "np"], xs[n, "nm"]] + xs[n, "v"])
        v = blk(q, a, 0, h)[...].astype(F32) + xv[n, 0].astype(F32) + xv[n, 1].astype(F32)
        if a:
            probe = (Wi if q else Wo)[rows(x * 2 + lo_of[h], R), B]
            v = scale * probe.astype(F32) * v
        v = v.astype(BF)
        o = 2 * (1 - q) + a
        if h:
            stage[o, :, mine] = v
        else:
            ys[o] = v
            xs[o, "y"] = send("y%d" % o, ys.at[o], stage.at[o, :, mine], mate)

    def sP(u):
        st[u]["c2"].wait_recv()
        for name in ("f1", "f2"):
            for cp in st[u][name]:
                cp.wait_send()
        for h in (0, 1):
            cols = rows(lo_of[h], H)
            g = dot_tn(err[u, :, cols], ad[:, B])
            if u >= 4:
                g = g + dot_tn(err[u - 4, :, cols], ad[:, A])
            sm[u, pl.ds(0, R), cols] = g.astype(BF)
            x_out(0, u // 4, u % 4, h)

    def sQ(u):
        st[u]["c2"].wait_recv()
        w = wrows(u)
        col = B if u >= 4 else A
        v = dot_nn(err[u], Wo[w, A])
        acc[:, col] = v if u in FIRST else acc[:, col] + v
        if u >= 4:
            acc[:, col] = acc[:, col] + dot_nn(err[u - 4], Wo[w, B])

    def pre_grad(a):
        @pl.loop(0, 2 * T // 128)
        def _(j):
            r = rows(j, 128)
            if a:
                ad[r, A] = (acc[r, B] * fg[r, A] + acc[r, A] * fg[r, B]).astype(BF)
            else:
                pg[r, :] = (acc[r, A] * fg[r, A]).astype(BF)

        for cp in r1[2 * a, 0] + r1[2 * a, 1] + r2[2 * a, 0] + r2[2 * a, 1]:
            cp.wait_send()

    def sN(n):
        a, i, h = n // 8, (n // 2) % 4, n % 2
        fc = pl.ds(al((chunk[i] % 4) * K + lo_of[h] * R, R), R)
        right = ad[:, A] if a else pg[...]
        blk(1, a, i, h)[...] = dot_tn(Tk[:, fc], right).astype(BF)
        x_out(1, a, i, h)

    def sF0(u):
        if u == 0:
            tg_loc.wait()
            tgx.wait_recv()
        sF(u)

    tasks = {
        "A": sA, "B": sB, "C": sC, "D": sD, "E": sE, "F": sF0, "G": sG, "H": sH, "I": sI, "J": sJ, "P": sP, "Q": sQ,
        "X": lambda n: ring1(n // 2, n % 2), "Y": lambda n: ring2(n // 2, n % 2), "M": tangent, "R": x_relay,
        "T": x_final, "W": pre_grad, "N": sN,
    }
    for step in ORDER:
        tasks[step[0]](int(step[1:]))
    got([xs[2, "y"], xs[3, "y"]])
    fin = [local(stage.at[2], out2), local(stage.at[3], out3)]
    got([xs[0, "y"], xs[1, "y"]])
    fin += [local(stage.at[0], out0), local(stage.at[1], out1)]
    for cp in started:
        cp.wait_send()
    for cp in fin:
        cp.wait()


def widen_kernel(*refs):
    for src, dst in zip(refs[:4], refs[4:]):
        dst[...] = src[...].astype(F32)


def on_device(tokens, target, w_in, probe_in, w_out, probe_out):
    R, hid = w_in.shape
    T, D = tokens.shape
    groups = lax.axis_size("replica")
    H, K, C = hid // 2, 2 * R, hid
    scale = float(T * groups) ** (-0.5)
    V = pltpu.VMEM
    scratch = [
        V((2 * T, D), BF),
        V((D, C), BF),
        V((D, C), BF),
        V((2 * T, C), F32),
        V((2 * T, C), BF),
        V((2 * T, C), F32),
        V((2 * T, H), BF),
        V((SLOTS, T, K), BF),
        V((8, T, K), BF),
        V((8, 2, T // 4, R), BF),
        V((8, 2, T // 4, K), BF),
        V((8, T // 4, K), BF),
        V((8, 2, T // 16, R), BF),
        V((8, 2, T // 16, K), BF),
        V((8, 2 * T, K), BF),
        V((8, 2, R // 2, H), BF),
        V((8, 2, R, H), BF),
        V((4, R, H), BF),
        V((4, R, C), BF),
        V((2, T // 16, D), BF),
        pltpu.SemaphoreType.DMA((12,)),
        pltpu.SemaphoreType.DMA((N_SEM,)),
        pltpu.SemaphoreType.DMA((N_SEM,)),
    ]
    res = pl.pallas_call(
        functools.partial(block_kernel, scale),
        out_shape=(jax.ShapeDtypeStruct((R, hid), BF),) * 4,
        in_specs=[pl.BlockSpec(memory_space=pl.ANY)] * 6,
        out_specs=(pl.BlockSpec(memory_space=pl.ANY),) * 4,
        scratch_shapes=scratch,
        compiler_params=pltpu.CompilerParams(collective_id=0, has_side_effects=True, vmem_limit_bytes=64 * 2**20),
        cost_estimate=pl.CostEstimate(flops=26 * T * D * hid, bytes_accessed=40 * 2**20, transcendentals=4 * T * H),
        name="sophia_block",
    )(tokens, target, w_in, probe_in, w_out, probe_out)
    block = pl.BlockSpec((R // 4, hid), lambda i: (i, 0))
    return pl.pallas_call(
        widen_kernel,
        grid=(4,),
        out_shape=(jax.ShapeDtypeStruct((R, hid), F32),) * 4,
        in_specs=[block] * 4,
        out_specs=(block,) * 4,
        cost_estimate=pl.CostEstimate(flops=0, bytes_accessed=24 * R * hid, transcendentals=0),
        name="widen",
    )(*res)


def solution(mesh):
    wide = P("replica", "shard")
    return jax.shard_map(
        on_device,
        mesh=mesh,
        in_specs=(P("replica", None), P("replica", None), wide, wide, wide, wide),
        out_specs=(wide, wide, wide, wide),
        check_vma=False,
    )
```
